768 devices in a mesh: dom: 192 (over z, y, core), grp: 4 (over x).
Axes of the slice: x: 4, y: 8, z: 12, core: 2. Of those that a mesh axis runs over, the one named last changes fastest.
Arguments:
- features: bfloat16 [393216, 512], P(('dom', 'grp')), may hold values from -6 to 6
- halo_in: bfloat16 [393216, 512], P(('dom', 'grp')), may hold values from -6 to 6
- neighbors: int32 [393216, 10], P(('dom', 'grp')), may hold values from 0 to 1023
- send_rows: int32 [393216], P(('dom', 'grp')), may hold values from 0 to 511
- grad_halo_in: bfloat16 [393216, 512], P(('dom', 'grp')), may hold values from -6 to 6
- out_grad: bfloat16 [393216, 512], P(('dom', 'grp')), may hold values from -6 to 6
- w_self: bfloat16 [512, 512], replicated, may hold values from -0.25 to 0.25
- w_neigh: bfloat16 [512, 512], replicated, may hold values from -0.25 to 0.25
Outputs:
- layer_out: bfloat16 [393216, 512], P(('dom', 'grp'))
- feat_grad: bfloat16 [393216, 512], P(('dom', 'grp'))
- next_halo: bfloat16 [393216, 512], P(('dom', 'grp'))
- next_grad_halo: bfloat16 [393216, 512], P(('dom', 'grp'))
- w_grads: float32 [2, 512, 512], replicated
The draws below stay inside these ranges and needn't reach their ends.
Inputs may be any that keep to these rules, and one draw needn't show every extreme that they name: `neighbors`: each entry names one of its partition's 512 own rows or 512 halo rows. `send_rows`: each entry names one of its partition's own rows.
All inputs are finite; a program needn't handle non-finite values.
Results may differ from the reference program's by a relative error of at most 0.005.
Values may be sent and summed in bfloat16 or wider, within the bound.
A program may use at most 32 MiB of HBM per device.

```python
import math
import jax
import jax.numpy as jnp
from jax import lax

H = 512
NODES_DEV = 512
BND = 128
FANOUT = 10
HALO = 512
NODES = 393216
N_DOM = 192
N_GRP = 4
DEVICES = 768


def with_ends(entries, key, least, top_value):
    index_at = [jax.random.randint(jax.random.fold_in(key, axis), (), 0, length) for axis, length in enumerate(entries.shape)]
    main_axis = entries.shape.index(max(entries.shape))
    neighbour = index_at[:main_axis] + [(index_at[main_axis] + 1) % entries.shape[main_axis]] + index_at[main_axis + 1:]
    return entries.at[tuple(index_at)].set(least).at[tuple(neighbour)].set(top_value)


def level_of(own_key, dims, cuts, low, largest):
    def one(position, shards_of):
        steps = jax.random.uniform(jax.random.fold_in(jax.random.fold_in(own_key, 6), position), (shards_of,), jnp.float32, low / len(cuts), largest / len(cuts))
        return jnp.repeat(jnp.exp(steps), dims[position] // shards_of).reshape((-1,) + (1,) * (len(dims) - position - 1))

    gain = one(*cuts[0])
    for cut in cuts[1:]:
        gain = gain * one(*cut)
    return gain


def normal_values(own_key, dims, width, most, shards=(), dtype=jnp.bfloat16):
    result = jax.random.normal(own_key, dims, jnp.float32) * width
    if len(shards) > 0:
        result = level_of(own_key, dims, shards, -0.22, 0.18) * result
    return jnp.clip(result, min=-most, max=most).astype(dtype)


def setup_inputs(seed: int = 0) -> dict:
    arg_keys = jax.random.split(jax.random.key(seed), 9)
    features = normal_values(arg_keys[0], (NODES, H), 1.0, 6.0, ((0, 768),))
    halo_in = normal_values(arg_keys[1], (DEVICES * HALO, H), 1.0, 6.0, ((0, 768),))
    neighbors = with_ends(jax.random.randint(arg_keys[2], (NODES, FANOUT), 0, NODES_DEV + HALO), jax.random.fold_in(arg_keys[2], 1), 0, (NODES_DEV + HALO) - 1).astype(jnp.int32)
    send_rows = with_ends(jax.random.randint(arg_keys[3], (DEVICES * HALO,), 0, NODES_DEV), jax.random.fold_in(arg_keys[3], 1), 0, NODES_DEV - 1).astype(jnp.int32)
    grad_halo_in = normal_values(arg_keys[4], (DEVICES * HALO, H), 1.0, 6.0, ((0, 768),))
    out_grad = normal_values(arg_keys[5], (NODES, H), 1.0, 6.0, ((0, 768),))
    w_self = normal_values(arg_keys[6], (H, H), H ** -0.5, 0.25)
    w_neigh = normal_values(arg_keys[7], (H, H), H ** -0.5, 0.25)
    return dict(features=features, halo_in=halo_in, neighbors=neighbors, send_rows=send_rows, grad_halo_in=grad_halo_in, out_grad=out_grad, w_self=w_self, w_neigh=w_neigh)


def partition_step(row_feats, row_halo, row_nbrs, row_send, row_gin, row_ograd, w_self, w_neigh):
    fanout = row_nbrs.shape[1]
    local_rows = row_feats.shape[0]
    row_table = jnp.concatenate([row_feats, row_halo], axis=0)
    gathered = row_table[row_nbrs]
    aggregate = (lax.optimization_barrier(jnp.sum(gathered.astype(jnp.float32), axis=1)) / fanout).astype(jnp.bfloat16)
    pre_act = jnp.dot(row_feats, w_self, preferred_element_type=jnp.float32) + jnp.dot(aggregate, w_neigh, preferred_element_type=jnp.float32)
    sigmoid = jax.nn.sigmoid(pre_act)
    layer_out = (pre_act * sigmoid).astype(jnp.bfloat16)
    act_grad = (row_ograd.astype(jnp.float32) * sigmoid * (1.0 + pre_act * (1.0 - sigmoid))).astype(jnp.bfloat16)
    wself_grad = jnp.dot(row_feats.T, act_grad, preferred_element_type=jnp.float32)
    wneigh_grad = jnp.dot(aggregate.T, act_grad, preferred_element_type=jnp.float32)
    self_grad = jnp.dot(act_grad, w_self.T, preferred_element_type=jnp.float32)
    neigh_grad = jnp.dot(act_grad, w_neigh.T, preferred_element_type=jnp.float32) / fanout
    indices = jnp.concatenate([row_nbrs.reshape(-1), row_send]).astype(jnp.int32)
    values = jnp.concatenate([jnp.repeat(neigh_grad, fanout, axis=0), row_gin.astype(jnp.float32)], axis=0)
    table_grad = jax.ops.segment_sum(values, indices, num_segments=local_rows + row_halo.shape[0])
    feat_grad = (self_grad + table_grad[:local_rows]).astype(jnp.bfloat16)
    halo_grad = table_grad[local_rows:].astype(jnp.bfloat16)
    sent_rows = row_feats[row_send]
    return (layer_out, feat_grad, halo_grad, sent_rows, wself_grad, wneigh_grad)

def swap_blocks(blocks):
    shaped = blocks.reshape(N_DOM, N_GRP, N_GRP, BND, H)
    return jnp.swapaxes(shaped, 1, 2).reshape(DEVICES * HALO, H)

def reference(features, halo_in, neighbors, send_rows, grad_halo_in, out_grad, w_self, w_neigh):
    stacked = (features.reshape(DEVICES, NODES_DEV, H), halo_in.reshape(DEVICES, HALO, H), neighbors.reshape(DEVICES, NODES_DEV, FANOUT), send_rows.reshape(DEVICES, HALO), grad_halo_in.reshape(DEVICES, HALO, H), out_grad.reshape(DEVICES, NODES_DEV, H))

    def visit(totals, pieces):
        layer_out, feat_grad, halo_grad, sent_rows, wself_grad, wneigh_grad = partition_step(*pieces, w_self, w_neigh)
        return ((totals[0] + wself_grad, totals[1] + wneigh_grad), (layer_out, feat_grad, halo_grad, sent_rows))
    start = (jnp.zeros((H, H), jnp.float32), jnp.zeros((H, H), jnp.float32))
    totals, outputs = lax.scan(visit, start, stacked)
    layer_out = outputs[0].reshape(NODES, H)
    feat_grad = outputs[1].reshape(NODES, H)
    next_grad_halo = swap_blocks(outputs[2])
    next_halo = swap_blocks(outputs[3])
    grad_scale = 1.0 / math.sqrt(NODES)
    w_grads = jnp.stack([totals[0], totals[1]]) * grad_scale
    return (layer_out, feat_grad, next_halo, next_grad_halo, w_grads)
```

```python
import functools
import math

import jax
import jax.numpy as jnp
from jax import lax
from jax.experimental import pallas as pl
from jax.experimental.pallas import tpu as pltpu
from jax.sharding import PartitionSpec as P

MESH = pl.DeviceIdType.MESH
NX, NY, NZ = 4, 8, 12
ROWS = 512
H = 512
FAN = 10
XB = ROWS // NX
YB = XB // NY
CH = 4
CW = H // CH
DIM0 = (((0,), (0,)), ((), ()))
DIM1 = (((1,), (1,)), ((), ()))
F32 = jnp.float32
BF16 = jnp.bfloat16


def kernel(
    scale,
    feat_hbm, halo_hbm, nbr_hbm, send_hbm, gin_hbm, ograd_hbm, ws_hbm, wn_hbm,
    layer_hbm, fgrad_hbm, nhalo_hbm, nghalo_hbm, wout_hbm,
    table, pair, nbr, send, gin, ograd, wself, wneigh,
    counts, select, act, layer, fgrad, hgrad, sent,
    wpart, crecv, s1, xsend, xrecv, s2, ysend, yrecv, zbuf, ag,
    lsem, osem, cs, cr, xs, xr, ys, yr, zs, zr, ays, ayr, axs, axr, acs, acr, hs, hr, gs, gr,
):
    dom = lax.axis_index("dom")
    g = lax.axis_index("grp")
    core = lax.rem(dom, 2)
    y = lax.rem(dom // 2, NY)
    z = dom // (2 * NY)

    def at_core():
        return (dom + 1 - 2 * core, g)

    def at_x(k):
        return (dom, lax.rem(g + k, NX))

    def at_y(k):
        return ((z * NY + lax.rem(y + k, NY)) * 2 + core, g)

    def at_z(k):
        return ((lax.rem(z + k, NZ) * NY + y) * 2 + core, g)

    barrier = pltpu.get_barrier_semaphore()
    peers = [at_core()] + [at_x(k) for k in range(1, NX)]
    peers += [at_y(k) for k in range(1, NY)] + [at_z(k) for k in range(1, NZ)]
    for peer in peers:
        pl.semaphore_signal(barrier, inc=1, device_id=peer, device_id_type=MESH)

    loads = [
        (nbr_hbm, nbr),
        (feat_hbm, table.at[pl.ds(0, ROWS)]),
        (halo_hbm, table.at[pl.ds(ROWS, ROWS)]),
        (ws_hbm, wself),
        (wn_hbm, wneigh),
        (ograd_hbm, ograd),
        (feat_hbm, pair.at[0]),
        (send_hbm, send),
        (gin_hbm, gin),
    ]
    copies = [pltpu.make_async_copy(s, d, lsem.at[i]) for i, (s, d) in enumerate(loads)]
    for copy in copies:
        copy.start()

    copies[0].wait()
    RB = 64
    ids = lax.broadcasted_iota(jnp.int32, (RB, 2 * ROWS), 1)

    @pl.loop(0, ROWS // RB)
    def _(b):
        rows = pl.ds(pl.multiple_of(b * RB, RB), RB)
        block = nbr[rows, :]
        total = jnp.zeros((RB, 2 * ROWS), F32)
        for slot in range(FAN):
            total = total + jnp.where(block[:, slot : slot + 1] == ids, 1.0, 0.0)
        counts[rows, :] = total.astype(BF16)

    for i in (1, 2, 3, 4, 5, 6):
        copies[i].wait()
    agg = jnp.dot(counts[...], table[...], preferred_element_type=F32) * (1.0 / FAN)
    pair[1] = agg.astype(BF16)
    pre = jnp.dot(table[pl.ds(0, ROWS), :], wself[...], preferred_element_type=F32)
    pre = pre + jnp.dot(pair[1], wneigh[...], preferred_element_type=F32)
    sig = jax.nn.sigmoid(pre)
    layer[...] = (pre * sig).astype(BF16)
    act[...] = (ograd[...].astype(F32) * sig * (1.0 + pre * (1.0 - sig))).astype(BF16)

    mine = core * ROWS
    other = ROWS - mine

    def cols(c):
        return pl.ds(c * CW, CW)

    def remote(src, dst, send_sem, recv_sem, device):
        copy = pltpu.make_async_remote_copy(
            src_ref=src, dst_ref=dst, send_sem=send_sem, recv_sem=recv_sem,
            device_id=device, device_id_type=MESH,
        )
        copy.start()

    def wait_for(ref, sem):
        pltpu.make_async_copy(ref, ref, sem).wait()

    wpart[1] = lax.dot_general(pair[1 - core], act[...], DIM0, preferred_element_type=F32)
    pl.semaphore_wait(barrier, len(peers))
    for c in range(CH):
        remote(wpart.at[1, :, cols(c)], crecv.at[:, cols(c)], cs.at[c], cr.at[c], at_core())
    wpart[0] = lax.dot_general(pair[core], act[...], DIM0, preferred_element_type=F32)
    out_layer = pltpu.make_async_copy(layer, layer_hbm, osem.at[0])
    out_layer.start()

    for c in range(CH):
        wait_for(crecv.at[:, cols(c)], cr.at[c])
        total = wpart[0, :, cols(c)] + crecv[:, cols(c)]
        s1[:, cols(c)] = total
        xsend[:, cols(c)] = total.astype(BF16)
        for k in range(1, NX):
            to = lax.rem(g + k, NX)
            rows = pl.ds(pl.multiple_of(to * XB, XB), XB)
            remote(xsend.at[rows, cols(c)], xrecv.at[c, k - 1], xs.at[c], xr.at[c], at_x(k))

    copies[7].wait()
    copies[8].wait()
    own_ids = lax.broadcasted_iota(jnp.int32, (ROWS, ROWS), 0)
    select[...] = jnp.where(own_ids == send[...], 1.0, 0.0).astype(BF16)
    sent[...] = lax.dot_general(
        select[...], table[pl.ds(0, ROWS), :], DIM0, preferred_element_type=F32
    ).astype(BF16)
    here = pl.ds(pl.multiple_of(g * XB, XB), XB)
    for k in range(1, NX):
        to = lax.rem(g + k, NX)
        rows = pl.ds(pl.multiple_of(to * XB, XB), XB)
        remote(sent.at[rows], nhalo_hbm.at[here], hs, hr, at_x(k))
    own_sent = pltpu.make_async_copy(sent.at[here], nhalo_hbm.at[here], osem.at[1])
    own_sent.start()

    for c in range(CH):
        wait_for(xrecv.at[c], xr.at[c])
        total = s1[here, cols(c)]
        for k in range(NX - 1):
            total = total + xrecv[c, k].astype(F32)
        s2[:, cols(c)] = total
        ysend[:, cols(c)] = total.astype(BF16)
        for k in range(1, NY):
            to = lax.rem(y + k, NY)
            rows = pl.ds(pl.multiple_of(to * YB, YB), YB)
            remote(
                ysend.at[rows, cols(c)], yrecv.at[c, pl.ds((k - 1) * YB, YB)],
                ys.at[c], yr.at[c], at_y(k),
            )

    grad = lax.dot_general(act[...], wneigh[...], DIM1, preferred_element_type=F32)
    grad = grad * (1.0 / FAN)
    high = grad.astype(BF16)
    low = (grad - high.astype(F32)).astype(BF16)
    back = lax.dot_general(
        counts[:, pl.ds(ROWS, ROWS)], high, DIM0, preferred_element_type=F32
    ) + lax.dot_general(counts[:, pl.ds(ROWS, ROWS)], low, DIM0, preferred_element_type=F32)
    hgrad[...] = back.astype(BF16)
    for k in range(1, NX):
        to = lax.rem(g + k, NX)
        rows = pl.ds(pl.multiple_of(to * XB, XB), XB)
        remote(hgrad.at[rows], nghalo_hbm.at[here], gs, gr, at_x(k))
    own_grad = pltpu.make_async_copy(hgrad.at[here], nghalo_hbm.at[here], osem.at[2])
    own_grad.start()

    own_y = pl.ds(pl.multiple_of(y * YB, YB), YB)
    own_z = pl.ds(pl.multiple_of(z * YB, YB), YB)
    for c in range(CH):
        wait_for(yrecv.at[c], yr.at[c])
        total = s2[own_y, cols(c)]
        for k in range(NY - 1):
            total = total + yrecv[c, pl.ds(k * YB, YB), :].astype(F32)
        zbuf[c, own_z, :] = total.astype(BF16)
        for k in range(1, NZ):
            remote(zbuf.at[c, own_z], zbuf.at[c, own_z], zs.at[c], zr.at[c], at_z(k))

    own = lax.dot_general(act[...], wself[...], DIM1, preferred_element_type=F32)
    own = own + lax.dot_general(
        counts[:, pl.ds(0, ROWS)], high, DIM0, preferred_element_type=F32
    )
    own = own + lax.dot_general(
        counts[:, pl.ds(0, ROWS)], low, DIM0, preferred_element_type=F32
    )
    own = own + jnp.dot(select[...], gin[...], preferred_element_type=F32)
    fgrad[...] = own.astype(BF16)
    out_fgrad = pltpu.make_async_copy(fgrad, fgrad_hbm, osem.at[3])
    out_fgrad.start()

    row_y = pl.ds(pl.multiple_of(mine + g * XB + y * YB, YB), YB)
    row_x = pl.ds(pl.multiple_of(mine + g * XB, XB), XB)
    row_c = pl.ds(pl.multiple_of(mine, ROWS), ROWS)
    row_o = pl.ds(pl.multiple_of(other, ROWS), ROWS)
    for c in range(CH):
        wait_for(zbuf.at[c, pl.ds(0, (NZ - 1) * YB)], zr.at[c])
        total = zbuf[c, pl.ds(0, YB), :].astype(F32)
        for k in range(1, NZ):
            total = total + zbuf[c, pl.ds(k * YB, YB), :].astype(F32)
        ag[row_y, cols(c)] = (total * scale).astype(BF16)
        for k in range(1, NY):
            remote(
                ag.at[row_y, cols(c)], ag.at[row_y, cols(c)], ays.at[c], ayr.at[c], at_y(k)
            )
    for c in range(CH):
        wait_for(ag.at[pl.ds(0, (NY - 1) * YB), cols(c)], ayr.at[c])
        for k in range(1, NX):
            remote(
                ag.at[row_x, cols(c)], ag.at[row_x, cols(c)], axs.at[c], axr.at[c], at_x(k)
            )
    for c in range(CH):
        wait_for(ag.at[pl.ds(0, (NX - 1) * XB), cols(c)], axr.at[c])
        remote(ag.at[row_c, cols(c)], ag.at[row_c, cols(c)], acs.at[c], acr.at[c], at_core())
    out_mine = pltpu.make_async_copy(ag.at[row_c], wout_hbm.at[row_c], osem.at[4])
    out_mine.start()
    for c in range(CH):
        wait_for(ag.at[row_o, cols(c)], acr.at[c])
    out_other = pltpu.make_async_copy(ag.at[row_o], wout_hbm.at[row_o], osem.at[5])
    out_other.start()

    wait_for(nhalo_hbm.at[pl.ds(0, ROWS - XB)], hr)
    wait_for(nghalo_hbm.at[pl.ds(0, ROWS - XB)], gr)
    wait_for(sent.at[pl.ds(0, ROWS - XB)], hs)
    wait_for(hgrad.at[pl.ds(0, ROWS - XB)], gs)
    for c in range(CH):
        wait_for(crecv.at[:, cols(c)], cs.at[c])
        wait_for(xrecv.at[c], xs.at[c])
        wait_for(yrecv.at[c], ys.at[c])
        wait_for(zbuf.at[c, pl.ds(0, (NZ - 1) * YB)], zs.at[c])
        wait_for(ag.at[pl.ds(0, (NY - 1) * YB), cols(c)], ays.at[c])
        wait_for(ag.at[pl.ds(0, (NX - 1) * XB), cols(c)], axs.at[c])
        wait_for(ag.at[row_c, cols(c)], acs.at[c])
    for copy in (out_layer, own_sent, own_grad, out_fgrad, out_mine, out_other):
        copy.wait()


def body(features, halo_in, neighbors, send_rows, grad_halo_in, out_grad, w_self, w_neigh):
    total_nodes = ROWS * lax.axis_size("dom") * lax.axis_size("grp")
    scale = 1.0 / math.sqrt(total_nodes)
    rows = jax.ShapeDtypeStruct((ROWS, H), BF16)
    anywhere = pl.BlockSpec(memory_space=pl.ANY)
    half = pltpu.VMEM((ROWS, H), BF16)
    dma = pltpu.SemaphoreType.DMA
    layer_out, feat_grad, next_halo, next_grad_halo, weights = pl.pallas_call(
        functools.partial(kernel, scale),
        out_shape=(rows, rows, rows, rows, jax.ShapeDtypeStruct((2 * ROWS, H), BF16)),
        in_specs=[anywhere] * 8,
        out_specs=(anywhere,) * 5,
        scratch_shapes=[
            pltpu.VMEM((2 * ROWS, H), BF16),
            pltpu.VMEM((2, ROWS, H), BF16),
            pltpu.VMEM((ROWS, FAN), jnp.int32),
            pltpu.VMEM((1, ROWS), jnp.int32),
            half, half, half, half,
            pltpu.VMEM((ROWS, 2 * ROWS), BF16),
            half, half, half, half, half, half,
            pltpu.VMEM((2, ROWS, H), F32),
            pltpu.VMEM((ROWS, H), F32),
            pltpu.VMEM((ROWS, H), F32),
            half,
            pltpu.VMEM((CH, NX - 1, XB, CW), BF16),
            pltpu.VMEM((XB, H), F32),
            pltpu.VMEM((XB, H), BF16),
            pltpu.VMEM((CH, (NY - 1) * YB, CW), BF16),
            pltpu.VMEM((CH, NZ * YB, CW), BF16),
            pltpu.VMEM((2 * ROWS, H), BF16),
            dma((9,)), dma((6,)),
        ] + [dma((CH,))] * 14 + [dma] * 4,
        compiler_params=pltpu.CompilerParams(
            collective_id=0, has_side_effects=True, vmem_limit_bytes=48 << 20
        ),
    )(
        features, halo_in, neighbors, send_rows.reshape(1, ROWS), grad_halo_in, out_grad,
        w_self, w_neigh,
    )
    w_grads = weights.astype(F32).reshape(2, ROWS, H)
    return layer_out, feat_grad, next_halo, next_grad_halo, w_grads


def solution(mesh):
    rows = P(("dom", "grp"), None)
    return jax.shard_map(
        body,
        mesh=mesh,
        in_specs=(rows, rows, rows, P(("dom", "grp")), rows, rows, P(), P()),
        out_specs=(rows, rows, rows, rows, P()),
        check_vma=False,
    )
```

```python
import functools
import math

import jax
import jax.numpy as jnp
from jax import lax
from jax.experimental import pallas as pl
from jax.experimental.pallas import tpu as pltpu
from jax.sharding import PartitionSpec as P

MESH = pl.DeviceIdType.MESH
NX, NY, NZ = 4, 8, 12
ROWS = 512
H = 512
FAN = 10
XB = ROWS // NX
YB = XB // NY
CH = 4
CW = H // CH
DIM0 = (((0,), (0,)), ((), ()))
DIM1 = (((1,), (1,)), ((), ()))
F32 = jnp.float32
BF16 = jnp.bfloat16


def kernel(
    scale,
    feat_hbm, halo_hbm, nbr_hbm, send_hbm, gin_hbm, ograd_hbm, ws_hbm, wn_hbm,
    layer, fgrad, nhalo, nghalo, ag,
    table, pair, nbr, send, gin, ograd, wself, wneigh,
    counts, select, act, hgrad, sent,
    wpart, crecv, s1, xsend, xrecv, s2, ysend, yrecv, zbuf,
    lsem, osem, cs, cr, xs, xr, ys, yr, zs, zr, ays, ayr, axs, axr, acs, acr, hs, hr, gs, gr,
):
    dom = lax.axis_index("dom")
    g = lax.axis_index("grp")
    core = lax.rem(dom, 2)
    y = lax.rem(dom // 2, NY)
    z = dom // (2 * NY)

    def at_core():
        return (dom + 1 - 2 * core, g)

    def at_x(k):
        return (dom, lax.rem(g + k, NX))

    def at_y(k):
        return ((z * NY + lax.rem(y + k, NY)) * 2 + core, g)

    def at_z(k):
        to = jnp.where(z >= k, k - 1, k)
        return ((to * NY + y) * 2 + core, g)

    barrier = pltpu.get_barrier_semaphore()
    peers = [at_core()] + [at_x(k) for k in range(1, NX)]
    peers += [at_y(k) for k in range(1, NY)] + [at_z(k) for k in range(1, NZ)]
    for peer in peers:
        pl.semaphore_signal(barrier, inc=1, device_id=peer, device_id_type=MESH)

    loads = [
        (nbr_hbm, nbr),
        (feat_hbm, table.at[pl.ds(0, ROWS)]),
        (halo_hbm, table.at[pl.ds(ROWS, ROWS)]),
        (ws_hbm, wself),
        (wn_hbm, wneigh),
        (ograd_hbm, ograd),
        (feat_hbm, pair.at[0]),
        (send_hbm, send),
        (gin_hbm, gin),
    ]
    copies = [pltpu.make_async_copy(s, d, lsem.at[i]) for i, (s, d) in enumerate(loads)]
    for copy in copies:
        copy.start()

    copies[0].wait()
    one = jnp.full((16, ROWS), 1, jnp.int16)
    none = jnp.zeros((16, ROWS), jnp.int16)
    slots = [
        jnp.broadcast_to(nbr[pl.ds(k, 1), :], (16, ROWS)).astype(jnp.int16) for k in range(FAN)
    ]
    ids = lax.broadcasted_iota(jnp.int32, (16, CW), 0)
    GROUP = 128

    @pl.loop(0, 2 * ROWS // GROUP)
    def _(b):
        for part in range(GROUP // 16):
            first = pl.multiple_of(b * GROUP + part * 16, 16)
            row_ids = jnp.tile((ids + first).astype(jnp.int16), (1, ROWS // CW))
            total = none
            for slot in slots:
                total = total + jnp.where(slot == row_ids, one, none)
            counts[pl.ds(first, 16), :] = total.astype(BF16)

    for i in (1, 2, 3, 4, 5, 6):
        copies[i].wait()
    agg = lax.dot_general(counts[...], table[...], DIM0, preferred_element_type=F32) * (1.0 / FAN)
    pair[1] = agg.astype(BF16)
    pre = jnp.dot(table[pl.ds(0, ROWS), :], wself[...], preferred_element_type=F32)
    pre = pre + jnp.dot(pair[1], wneigh[...], preferred_element_type=F32)
    sig = jax.nn.sigmoid(pre)
    layer[...] = (pre * sig).astype(BF16)
    act[...] = (ograd[...].astype(F32) * sig * (1.0 + pre * (1.0 - sig))).astype(BF16)

    mine = core * ROWS
    other = ROWS - mine

    def cols(c):
        return pl.ds(c * CW, CW)

    def remote(src, dst, send_sem, recv_sem, device):
        copy = pltpu.make_async_remote_copy(
            src_ref=src, dst_ref=dst, send_sem=send_sem, recv_sem=recv_sem,
            device_id=device, device_id_type=MESH,
        )
        copy.start()

    def wait_for(ref, sem):
        pltpu.make_async_copy(ref, ref, sem).wait()

    wpart[1] = lax.dot_general(pair[1 - core], act[...], DIM0, preferred_element_type=F32)
    pl.semaphore_wait(barrier, len(peers))
    for c in range(CH):
        remote(wpart.at[1, :, cols(c)], crecv.at[:, cols(c)], cs.at[c], cr.at[c], at_core())
    wpart[0] = lax.dot_general(pair[core], act[...], DIM0, preferred_element_type=F32)

    for c in range(CH):
        wait_for(crecv.at[:, cols(c)], cr.at[c])
        total = wpart[0, :, cols(c)] + crecv[:, cols(c)]
        s1[:, cols(c)] = total
        xsend[:, cols(c)] = total.astype(BF16)
        for k in range(1, NX):
            to = lax.rem(g + k, NX)
            rows = pl.ds(pl.multiple_of(to * XB, XB), XB)
            remote(xsend.at[rows, cols(c)], xrecv.at[c, k - 1], xs.at[c], xr.at[c], at_x(k))

    copies[7].wait()
    copies[8].wait()
    own_ids = lax.broadcasted_iota(jnp.int32, (ROWS, ROWS), 0)
    select[...] = jnp.where(own_ids == send[...], 1.0, 0.0).astype(BF16)
    sent[...] = lax.dot_general(
        select[...], table[pl.ds(0, ROWS), :], DIM0, preferred_element_type=F32
    ).astype(BF16)
    here = pl.ds(pl.multiple_of(g * XB, XB), XB)
    for k in range(1, NX):
        to = lax.rem(g + k, NX)
        rows = pl.ds(pl.multiple_of(to * XB, XB), XB)
        remote(sent.at[rows], nhalo.at[here], hs, hr, at_x(k))
    own_sent = pltpu.make_async_copy(sent.at[here], nhalo.at[here], osem.at[0])
    own_sent.start()

    for c in range(CH):
        wait_for(xrecv.at[c], xr.at[c])
        total = s1[here, cols(c)]
        for k in range(NX - 1):
            total = total + xrecv[c, k].astype(F32)
        s2[:, cols(c)] = total
        ysend[:, cols(c)] = total.astype(BF16)
        for k in range(1, NY):
            to = lax.rem(y + k, NY)
            rows = pl.ds(pl.multiple_of(to * YB, YB), YB)
            remote(
                ysend.at[rows, cols(c)], yrecv.at[c, pl.ds((k - 1) * YB, YB)],
                ys.at[c], yr.at[c], at_y(k),
            )

    grad = lax.dot_general(act[...], wneigh[...], DIM1, preferred_element_type=F32)
    grad = grad * (1.0 / FAN)
    high = grad.astype(BF16)
    low = (grad - high.astype(F32)).astype(BF16)
    halo_counts = counts[pl.ds(ROWS, ROWS), :]
    back = jnp.dot(halo_counts, high, preferred_element_type=F32)
    back = back + jnp.dot(halo_counts, low, preferred_element_type=F32)
    hgrad[...] = back.astype(BF16)
    for k in range(1, NX):
        to = lax.rem(g + k, NX)
        rows = pl.ds(pl.multiple_of(to * XB, XB), XB)
        remote(hgrad.at[rows], nghalo.at[here], gs, gr, at_x(k))
    own_grad = pltpu.make_async_copy(hgrad.at[here], nghalo.at[here], osem.at[1])
    own_grad.start()

    own_y = pl.ds(pl.multiple_of(y * YB, YB), YB)
    own_z = pl.ds(pl.multiple_of(z * YB, YB), YB)
    for c in range(CH):
        wait_for(yrecv.at[c], yr.at[c])
        total = s2[own_y, cols(c)]
        for k in range(NY - 1):
            total = total + yrecv[c, pl.ds(k * YB, YB), :].astype(F32)
        zbuf[c, own_z, :] = total.astype(BF16)
        for k in range(1, NZ):
            remote(zbuf.at[c, own_z], zbuf.at[c, own_z], zs.at[c], zr.at[c], at_z(k))

    own = lax.dot_general(act[...], wself[...], DIM1, preferred_element_type=F32)
    own_counts = counts[pl.ds(0, ROWS), :]
    own = own + jnp.dot(own_counts, high, preferred_element_type=F32)
    own = own + jnp.dot(own_counts, low, preferred_element_type=F32)
    own = own + jnp.dot(select[...], gin[...], preferred_element_type=F32)
    fgrad[...] = own.astype(BF16)

    row_y = pl.ds(pl.multiple_of(mine + g * XB + y * YB, YB), YB)
    row_x = pl.ds(pl.multiple_of(mine + g * XB, XB), XB)
    row_c = pl.ds(pl.multiple_of(mine, ROWS), ROWS)
    row_o = pl.ds(pl.multiple_of(other, ROWS), ROWS)
    for c in range(CH):
        wait_for(zbuf.at[c, pl.ds(0, (NZ - 1) * YB)], zr.at[c])
        total = zbuf[c, pl.ds(0, YB), :].astype(F32)
        for k in range(1, NZ):
            total = total + zbuf[c, pl.ds(k * YB, YB), :].astype(F32)
        ag[row_y, cols(c)] = (total * scale).astype(BF16)
        for k in range(1, NY):
            remote(
                ag.at[row_y, cols(c)], ag.at[row_y, cols(c)], ays.at[c], ayr.at[c], at_y(k)
            )
    for c in range(CH):
        wait_for(ag.at[pl.ds(0, (NY - 1) * YB), cols(c)], ayr.at[c])
        for k in range(1, NX):
            remote(
                ag.at[row_x, cols(c)], ag.at[row_x, cols(c)], axs.at[c], axr.at[c], at_x(k)
            )
    for c in range(CH):
        wait_for(ag.at[pl.ds(0, (NX - 1) * XB), cols(c)], axr.at[c])
        remote(ag.at[row_c, cols(c)], ag.at[row_c, cols(c)], acs.at[c], acr.at[c], at_core())
    for c in range(CH):
        wait_for(ag.at[row_o, cols(c)], acr.at[c])

    wait_for(nhalo.at[pl.ds(0, ROWS - XB)], hr)
    wait_for(nghalo.at[pl.ds(0, ROWS - XB)], gr)
    wait_for(sent.at[pl.ds(0, ROWS - XB)], hs)
    wait_for(hgrad.at[pl.ds(0, ROWS - XB)], gs)
    for c in range(CH):
        wait_for(crecv.at[:, cols(c)], cs.at[c])
        wait_for(xrecv.at[c], xs.at[c])
        wait_for(yrecv.at[c], ys.at[c])
        wait_for(zbuf.at[c, pl.ds(0, (NZ - 1) * YB)], zs.at[c])
        wait_for(ag.at[pl.ds(0, (NY - 1) * YB), cols(c)], ays.at[c])
        wait_for(ag.at[pl.ds(0, (NX - 1) * XB), cols(c)], axs.at[c])
        wait_for(ag.at[row_c, cols(c)], acs.at[c])
    for copy in (own_sent, own_grad):
        copy.wait()


def deliver(layer, fgrad, nhalo, nghalo, ag, o_layer, o_fgrad, o_nhalo, o_nghalo, o_w, wide, sems, wsems):
    pairs = ((layer, o_layer), (fgrad, o_fgrad), (nhalo, o_nhalo), (nghalo, o_nghalo))
    copies = [pltpu.make_async_copy(s, d, sems.at[i]) for i, (s, d) in enumerate(pairs)]
    for copy in copies:
        copy.start()
    pieces = wsems.shape[1]
    size = ROWS // pieces
    for m in range(2):
        for q in range(pieces):
            rows = pl.ds(q * size, size)
            wide[m, rows, :] = ag[pl.ds(m * ROWS + q * size, size), :].astype(F32)
            copies.append(
                pltpu.make_async_copy(wide.at[m, rows], o_w.at[m, rows], wsems.at[m, q])
            )
            copies[-1].start()
    for copy in copies:
        copy.wait()


def body(features, halo_in, neighbors, send_rows, grad_halo_in, out_grad, w_self, w_neigh):
    total_nodes = ROWS * lax.axis_size("dom") * lax.axis_size("grp")
    scale = 1.0 / math.sqrt(total_nodes)
    inside = pl.BlockSpec(memory_space=pltpu.VMEM)
    outside = pl.BlockSpec(memory_space=pltpu.HBM)
    half = pltpu.VMEM((ROWS, H), BF16)
    dma = pltpu.SemaphoreType.DMA
    args = [
        features, halo_in, neighbors.T, send_rows.reshape(1, ROWS), grad_halo_in, out_grad,
        w_self, w_neigh,
    ]
    results = pl.pallas_call(
        functools.partial(kernel, scale),
        out_shape=(half, half, half, half, pltpu.VMEM((2 * ROWS, H), BF16)),
        in_specs=[outside] * 8,
        out_specs=(inside,) * 5,
        scratch_shapes=[
            pltpu.VMEM((2 * ROWS, H), BF16),
            pltpu.VMEM((2, ROWS, H), BF16),
            pltpu.VMEM((FAN, ROWS), jnp.int32),
            pltpu.VMEM((1, ROWS), jnp.int32),
            half, half, half, half,
            pltpu.VMEM((2 * ROWS, ROWS), BF16),
            half, half, half, half,
            pltpu.VMEM((2, ROWS, H), F32),
            pltpu.VMEM((ROWS, H), F32),
            pltpu.VMEM((ROWS, H), F32),
            half,
            pltpu.VMEM((CH, NX - 1, XB, CW), BF16),
            pltpu.VMEM((XB, H), F32),
            pltpu.VMEM((XB, H), BF16),
            pltpu.VMEM((CH, (NY - 1) * YB, CW), BF16),
            pltpu.VMEM((CH, NZ * YB, CW), BF16),
            dma((9,)), dma((2,)),
        ] + [dma((CH,))] * 14 + [dma] * 4,
        compiler_params=pltpu.CompilerParams(
            collective_id=0, has_side_effects=True, vmem_limit_bytes=48 << 20
        ),
    )(*[pltpu.with_memory_space_constraint(a, pltpu.HBM) for a in args])
    rows = jax.ShapeDtypeStruct((ROWS, H), BF16)
    pieces = 4
    return pl.pallas_call(
        deliver,
        out_shape=(rows, rows, rows, rows, jax.ShapeDtypeStruct((2, ROWS, H), F32)),
        in_specs=[inside] * 5,
        out_specs=(outside,) * 5,
        scratch_shapes=[pltpu.VMEM((2, ROWS, H), F32), dma((4,)), dma((2, pieces))],
        compiler_params=pltpu.CompilerParams(vmem_limit_bytes=16 << 20),
    )(*[pltpu.with_memory_space_constraint(a, pltpu.VMEM) for a in results])


def solution(mesh):
    rows = P(("dom", "grp"), None)
    return jax.shard_map(
        body,
        mesh=mesh,
        in_specs=(rows, rows, rows, P(("dom", "grp")), rows, rows, P(), P()),
        out_specs=(rows, rows, rows, rows, P()),
        check_vma=False,
    )
```

```python
import functools
import math

import jax
import jax.numpy as jnp
from jax import lax
from jax.experimental import pallas as pl
from jax.experimental.pallas import tpu as pltpu
from jax.sharding import PartitionSpec as P

MESH = pl.DeviceIdType.MESH
NX, NY, NZ = 4, 8, 12
ROWS = 512
H = 512
FAN = 10
XB = ROWS // NX
YB = XB // NY
CH = 4
FIRST = 2
FAR_X = (2, 1, 3)
FAR_Y = (4, 3, 5, 2, 6, 1, 7)
CW = H // CH
DIM0 = (((0,), (0,)), ((), ()))
DIM1 = (((1,), (1,)), ((), ()))
F32 = jnp.float32
BF16 = jnp.bfloat16


def kernel(
    scale,
    feat_hbm, halo_hbm, nbr_hbm, send_hbm, gin_hbm, ograd_hbm, ws_hbm, wn_hbm,
    layer, fgrad, nhalo, nghalo, ag,
    table, pair, nbr, send, gin, ograd, wself, wneigh,
    counts, select, act, hgrad, sent,
    wpart, crecv, s1, xsend, xrecv, s2, ysend, yrecv, zbuf,
    lsem, osem, cs, cr, xs, xr, ys, yr, zs, zr, ays, ayr, axs, axr, acs, acr, hs, hr, gs, gr,
):
    dom = lax.axis_index("dom")
    g = lax.axis_index("grp")
    core = lax.rem(dom, 2)
    y = lax.rem(dom // 2, NY)
    z = dom // (2 * NY)

    def at_core():
        return (dom + 1 - 2 * core, g)

    def at_x(k):
        return (dom, lax.rem(g + k, NX))

    def at_y(k):
        return ((z * NY + lax.rem(y + k, NY)) * 2 + core, g)

    def at_z(k):
        to = jnp.where(z >= k, k - 1, k)
        return ((to * NY + y) * 2 + core, g)

    barrier = pltpu.get_barrier_semaphore()
    peers = [at_core()] + [at_x(k) for k in range(1, NX)]
    peers += [at_y(k) for k in range(1, NY)] + [at_z(k) for k in range(1, NZ)]
    for peer in peers:
        pl.semaphore_signal(barrier, inc=1, device_id=peer, device_id_type=MESH)

    loads = [
        (nbr_hbm, nbr),
        (feat_hbm, table.at[pl.ds(0, ROWS)]),
        (halo_hbm, table.at[pl.ds(ROWS, ROWS)]),
        (ws_hbm, wself),
        (wn_hbm, wneigh),
        (ograd_hbm, ograd),
        (feat_hbm, pair.at[0]),
        (send_hbm, send),
        (gin_hbm, gin),
    ]
    copies = [pltpu.make_async_copy(s, d, lsem.at[i]) for i, (s, d) in enumerate(loads)]
    for copy in copies:
        copy.start()

    copies[0].wait()
    one = jnp.full((16, ROWS), 1, jnp.int16)
    none = jnp.zeros((16, ROWS), jnp.int16)
    slots = [
        jnp.broadcast_to(nbr[pl.ds(k, 1), :], (16, ROWS)).astype(jnp.int16) for k in range(FAN)
    ]
    ids = lax.broadcasted_iota(jnp.int32, (16, 128), 0)
    GROUP = 128

    @pl.loop(0, 2 * ROWS // GROUP)
    def _(b):
        for part in range(GROUP // 16):
            first = pl.multiple_of(b * GROUP + part * 16, 16)
            row_ids = jnp.tile((ids + first).astype(jnp.int16), (1, ROWS // 128))
            total = none
            for slot in slots:
                total = total + jnp.where(slot == row_ids, one, none)
            counts[pl.ds(first, 16), :] = total.astype(BF16)

    for i in (1, 2, 3, 4, 5, 6):
        copies[i].wait()
    agg = lax.dot_general(counts[...], table[...], DIM0, preferred_element_type=F32) * (1.0 / FAN)
    pair[1] = agg.astype(BF16)
    pre = jnp.dot(table[pl.ds(0, ROWS), :], wself[...], preferred_element_type=F32)
    pre = pre + jnp.dot(pair[1], wneigh[...], preferred_element_type=F32)
    sig = jax.nn.sigmoid(pre)
    layer[...] = (pre * sig).astype(BF16)
    act[...] = (ograd[...].astype(F32) * sig * (1.0 + pre * (1.0 - sig))).astype(BF16)

    mine = core * ROWS
    other = ROWS - mine

    def cols(c):
        return pl.ds(c * CW, CW)

    def remote(src, dst, send_sem, recv_sem, device):
        copy = pltpu.make_async_remote_copy(
            src_ref=src, dst_ref=dst, send_sem=send_sem, recv_sem=recv_sem,
            device_id=device, device_id_type=MESH,
        )
        copy.start()

    def wait_for(ref, sem):
        pltpu.make_async_copy(ref, ref, sem).wait()

    wpart[1] = lax.dot_general(pair[1 - core], act[...], DIM0, preferred_element_type=F32)
    pl.semaphore_wait(barrier, len(peers))
    for c in range(CH):
        remote(wpart.at[1, :, cols(c)], crecv.at[:, cols(c)], cs.at[c], cr.at[c], at_core())
    wpart[0] = lax.dot_general(pair[core], act[...], DIM0, preferred_element_type=F32)

    for c in range(CH):
        wait_for(crecv.at[:, cols(c)], cr.at[c])
        total = wpart[0, :, cols(c)] + crecv[:, cols(c)]
        s1[:, cols(c)] = total
        xsend[:, cols(c)] = total.astype(BF16)
        for k in FAR_X:
            to = lax.rem(g + k, NX)
            rows = pl.ds(pl.multiple_of(to * XB, XB), XB)
            remote(xsend.at[rows, cols(c)], xrecv.at[c, k - 1], xs.at[c], xr.at[c], at_x(k))

    copies[7].wait()
    copies[8].wait()
    own_ids = lax.broadcasted_iota(jnp.int32, (ROWS, ROWS), 0)
    select[...] = jnp.where(own_ids == send[...], 1.0, 0.0).astype(BF16)
    sent[...] = lax.dot_general(
        select[...], table[pl.ds(0, ROWS), :], DIM0, preferred_element_type=F32
    ).astype(BF16)
    here = pl.ds(pl.multiple_of(g * XB, XB), XB)
    for k in range(1, NX):
        to = lax.rem(g + k, NX)
        rows = pl.ds(pl.multiple_of(to * XB, XB), XB)
        remote(sent.at[rows], nhalo.at[here], hs, hr, at_x(k))
    own_sent = pltpu.make_async_copy(sent.at[here], nhalo.at[here], osem.at[0])
    own_sent.start()

    for c in range(CH):
        wait_for(xrecv.at[c], xr.at[c])
        total = s1[here, cols(c)]
        for k in range(NX - 1):
            total = total + xrecv[c, k].astype(F32)
        s2[:, cols(c)] = total
        ysend[:, cols(c)] = total.astype(BF16)
        for k in FAR_Y:
            to = lax.rem(y + k, NY)
            rows = pl.ds(pl.multiple_of(to * YB, YB), YB)
            remote(
                ysend.at[rows, cols(c)], yrecv.at[c, pl.ds((k - 1) * YB, YB)],
                ys.at[c], yr.at[c], at_y(k),
            )

    grad = lax.dot_general(act[...], wneigh[...], DIM1, preferred_element_type=F32)
    grad = grad * (1.0 / FAN)
    high = grad.astype(BF16)
    low = (grad - high.astype(F32)).astype(BF16)
    halo_counts = counts[pl.ds(ROWS, ROWS), :]
    back = jnp.dot(halo_counts, high, preferred_element_type=F32)
    back = back + jnp.dot(halo_counts, low, preferred_element_type=F32)
    hgrad[...] = back.astype(BF16)
    for k in range(1, NX):
        to = lax.rem(g + k, NX)
        rows = pl.ds(pl.multiple_of(to * XB, XB), XB)
        remote(hgrad.at[rows], nghalo.at[here], gs, gr, at_x(k))
    own_grad = pltpu.make_async_copy(hgrad.at[here], nghalo.at[here], osem.at[1])
    own_grad.start()

    own_y = pl.ds(pl.multiple_of(y * YB, YB), YB)
    own_z = pl.ds(pl.multiple_of(z * YB, YB), YB)
    for c in range(CH):
        wait_for(yrecv.at[c], yr.at[c])
        total = s2[own_y, cols(c)]
        for k in range(NY - 1):
            total = total + yrecv[c, pl.ds(k * YB, YB), :].astype(F32)
        zbuf[c, own_z, :] = total.astype(BF16)
        for k in range(1, FIRST + 1):
            remote(zbuf.at[c, own_z], zbuf.at[c, own_z], zs.at[c], zr.at[c], at_z(k))
    for c in range(CH):
        for k in range(FIRST + 1, NZ):
            remote(zbuf.at[c, own_z], zbuf.at[c, own_z], zs.at[c], zr.at[c], at_z(k))

    own = lax.dot_general(act[...], wself[...], DIM1, preferred_element_type=F32)
    own_counts = counts[pl.ds(0, ROWS), :]
    own = own + jnp.dot(own_counts, high, preferred_element_type=F32)
    own = own + jnp.dot(own_counts, low, preferred_element_type=F32)
    own = own + jnp.dot(select[...], gin[...], preferred_element_type=F32)
    fgrad[...] = own.astype(BF16)

    row_y = pl.ds(pl.multiple_of(mine + g * XB + y * YB, YB), YB)
    row_x = pl.ds(pl.multiple_of(mine + g * XB, XB), XB)
    row_c = pl.ds(pl.multiple_of(mine, ROWS), ROWS)
    row_o = pl.ds(pl.multiple_of(other, ROWS), ROWS)
    for c in range(CH):
        wait_for(zbuf.at[c, pl.ds(0, (NZ - 1) * YB)], zr.at[c])
        total = zbuf[c, pl.ds(0, YB), :].astype(F32)
        for k in range(1, NZ):
            total = total + zbuf[c, pl.ds(k * YB, YB), :].astype(F32)
        ag[row_y, cols(c)] = (total * scale).astype(BF16)
        for k in FAR_Y:
            remote(
                ag.at[row_y, cols(c)], ag.at[row_y, cols(c)], ays.at[c], ayr.at[c], at_y(k)
            )
    for c in range(CH):
        wait_for(ag.at[pl.ds(0, (NY - 1) * YB), cols(c)], ayr.at[c])
        for k in FAR_X:
            remote(
                ag.at[row_x, cols(c)], ag.at[row_x, cols(c)], axs.at[c], axr.at[c], at_x(k)
            )
    for c in range(CH):
        wait_for(ag.at[pl.ds(0, (NX - 1) * XB), cols(c)], axr.at[c])
        remote(ag.at[row_c, cols(c)], ag.at[row_c, cols(c)], acs.at[c], acr.at[c], at_core())
    for c in range(CH):
        wait_for(ag.at[row_o, cols(c)], acr.at[c])

    wait_for(nhalo.at[pl.ds(0, ROWS - XB)], hr)
    wait_for(nghalo.at[pl.ds(0, ROWS - XB)], gr)
    wait_for(sent.at[pl.ds(0, ROWS - XB)], hs)
    wait_for(hgrad.at[pl.ds(0, ROWS - XB)], gs)
    for c in range(CH):
        wait_for(crecv.at[:, cols(c)], cs.at[c])
        wait_for(xrecv.at[c], xs.at[c])
        wait_for(yrecv.at[c], ys.at[c])
        wait_for(zbuf.at[c, pl.ds(0, (NZ - 1) * YB)], zs.at[c])
        wait_for(ag.at[pl.ds(0, (NY - 1) * YB), cols(c)], ays.at[c])
        wait_for(ag.at[pl.ds(0, (NX - 1) * XB), cols(c)], axs.at[c])
        wait_for(ag.at[row_c, cols(c)], acs.at[c])
    for copy in (own_sent, own_grad):
        copy.wait()


def deliver(layer, fgrad, nhalo, nghalo, ag, o_layer, o_fgrad, o_nhalo, o_nghalo, o_w, wide, sems, wsems):
    pairs = ((layer, o_layer), (fgrad, o_fgrad), (nhalo, o_nhalo), (nghalo, o_nghalo))
    copies = [pltpu.make_async_copy(s, d, sems.at[i]) for i, (s, d) in enumerate(pairs)]
    for copy in copies:
        copy.start()
    pieces = wsems.shape[1]
    size = ROWS // pieces
    for m in range(2):
        for q in range(pieces):
            rows = pl.ds(q * size, size)
            wide[m, rows, :] = ag[pl.ds(m * ROWS + q * size, size), :].astype(F32)
            copies.append(
                pltpu.make_async_copy(wide.at[m, rows], o_w.at[m, rows], wsems.at[m, q])
            )
            copies[-1].start()
    for copy in copies:
        copy.wait()


def body(features, halo_in, neighbors, send_rows, grad_halo_in, out_grad, w_self, w_neigh):
    total_nodes = ROWS * lax.axis_size("dom") * lax.axis_size("grp")
    scale = 1.0 / math.sqrt(total_nodes)
    inside = pl.BlockSpec(memory_space=pltpu.VMEM)
    outside = pl.BlockSpec(memory_space=pltpu.HBM)
    half = pltpu.VMEM((ROWS, H), BF16)
    dma = pltpu.SemaphoreType.DMA
    args = [
        features, halo_in, neighbors.T, send_rows.reshape(1, ROWS), grad_halo_in, out_grad,
        w_self, w_neigh,
    ]
    results = pl.pallas_call(
        functools.partial(kernel, scale),
        out_shape=(half, half, half, half, pltpu.VMEM((2 * ROWS, H), BF16)),
        in_specs=[outside] * 8,
        out_specs=(inside,) * 5,
        scratch_shapes=[
            pltpu.VMEM((2 * ROWS, H), BF16),
            pltpu.VMEM((2, ROWS, H), BF16),
            pltpu.VMEM((FAN, ROWS), jnp.int32),
            pltpu.VMEM((1, ROWS), jnp.int32),
            half, half, half, half,
            pltpu.VMEM((2 * ROWS, ROWS), BF16),
            half, half, half, half,
            pltpu.VMEM((2, ROWS, H), F32),
            pltpu.VMEM((ROWS, H), F32),
            pltpu.VMEM((ROWS, H), F32),
            half,
            pltpu.VMEM((CH, NX - 1, XB, CW), BF16),
            pltpu.VMEM((XB, H), F32),
            pltpu.VMEM((XB, H), BF16),
            pltpu.VMEM((CH, (NY - 1) * YB, CW), BF16),
            pltpu.VMEM((CH, NZ * YB, CW), BF16),
            dma((9,)), dma((2,)),
        ] + [dma((CH,))] * 14 + [dma] * 4,
        compiler_params=pltpu.CompilerParams(
            collective_id=0, has_side_effects=True, vmem_limit_bytes=48 << 20
        ),
    )(*[pltpu.with_memory_space_constraint(a, pltpu.HBM) for a in args])
    rows = jax.ShapeDtypeStruct((ROWS, H), BF16)
    pieces = 4
    return pl.pallas_call(
        deliver,
        out_shape=(rows, rows, rows, rows, jax.ShapeDtypeStruct((2, ROWS, H), F32)),
        in_specs=[inside] * 5,
        out_specs=(outside,) * 5,
        scratch_shapes=[pltpu.VMEM((2, ROWS, H), F32), dma((4,)), dma((2, pieces))],
        compiler_params=pltpu.CompilerParams(vmem_limit_bytes=16 << 20),
    )(*[pltpu.with_memory_space_constraint(a, pltpu.VMEM) for a in results])


def solution(mesh):
    rows = P(("dom", "grp"), None)
    return jax.shard_map(
        body,
        mesh=mesh,
        in_specs=(rows, rows, rows, P(("dom", "grp")), rows, rows, P(), P()),
        out_specs=(rows, rows, rows, rows, P()),
        check_vma=False,
    )
```

```python
import functools
import math

import jax
import jax.numpy as jnp
from jax import lax
from jax.experimental import pallas as pl
from jax.experimental.pallas import tpu as pltpu
from jax.sharding import PartitionSpec as P

MESH = pl.DeviceIdType.MESH
NX, NY, NZ = 4, 8, 12
ROWS = 512
H = 512
FAN = 10
XB = ROWS // NX
YB = XB // NY
WIDTHS = (128, 256, 128)
CH = len(WIDTHS)
FIRST = 2
FAR_X = (2, 1, 3)
FAR_Y = (4, 3, 5, 2, 6, 1, 7)
DIM0 = (((0,), (0,)), ((), ()))
DIM1 = (((1,), (1,)), ((), ()))
F32 = jnp.float32
BF16 = jnp.bfloat16


def kernel(
    scale,
    feat_hbm, halo_hbm, nbr_hbm, send_hbm, gin_hbm, ograd_hbm, ws_hbm, wn_hbm,
    layer, fgrad, nhalo, nghalo, ag,
    table, pair, nbr, send, gin, ograd, wself, wneigh,
    counts, select, act, hgrad, sent,
    wpart, crecv, s1, xsend, xrecv, s2, ysend, yrecv, zbuf,
    lsem, osem, cs, cr, xs, xr, ys, yr, zs, zr, ays, ayr, axs, axr, acs, acr, hs, hr, gs, gr,
):
    dom = lax.axis_index("dom")
    g = lax.axis_index("grp")
    core = lax.rem(dom, 2)
    y = lax.rem(dom // 2, NY)
    z = dom // (2 * NY)

    def at_core():
        return (dom + 1 - 2 * core, g)

    def at_x(k):
        return (dom, lax.rem(g + k, NX))

    def at_y(k):
        return ((z * NY + lax.rem(y + k, NY)) * 2 + core, g)

    def at_z(k):
        to = jnp.where(z >= k, k - 1, k)
        return ((to * NY + y) * 2 + core, g)

    barrier = pltpu.get_barrier_semaphore()
    peers = [at_core()] + [at_x(k) for k in range(1, NX)]
    peers += [at_y(k) for k in range(1, NY)] + [at_z(k) for k in range(1, NZ)]
    for peer in peers:
        pl.semaphore_signal(barrier, inc=1, device_id=peer, device_id_type=MESH)

    loads = [
        (nbr_hbm, nbr),
        (feat_hbm, table.at[pl.ds(0, ROWS)]),
        (halo_hbm, table.at[pl.ds(ROWS, ROWS)]),
        (ws_hbm, wself),
        (wn_hbm, wneigh),
        (ograd_hbm, ograd),
        (feat_hbm, pair.at[0]),
        (send_hbm, send),
        (gin_hbm, gin),
    ]
    copies = [pltpu.make_async_copy(s, d, lsem.at[i]) for i, (s, d) in enumerate(loads)]
    for copy in copies:
        copy.start()

    copies[0].wait()
    one = jnp.full((16, ROWS), 1, jnp.int16)
    none = jnp.zeros((16, ROWS), jnp.int16)
    slots = [
        jnp.broadcast_to(nbr[pl.ds(k, 1), :], (16, ROWS)).astype(jnp.int16) for k in range(FAN)
    ]
    ids = lax.broadcasted_iota(jnp.int32, (16, 128), 0)
    GROUP = 128

    @pl.loop(0, 2 * ROWS // GROUP)
    def _(b):
        for part in range(GROUP // 16):
            first = pl.multiple_of(b * GROUP + part * 16, 16)
            row_ids = jnp.tile((ids + first).astype(jnp.int16), (1, ROWS // 128))
            total = none
            for slot in slots:
                total = total + jnp.where(slot == row_ids, one, none)
            counts[pl.ds(first, 16), :] = total.astype(BF16)

    for i in (1, 2, 3, 4, 5, 6):
        copies[i].wait()
    agg = lax.dot_general(counts[...], table[...], DIM0, preferred_element_type=F32) * (1.0 / FAN)
    pair[1] = agg.astype(BF16)
    pre = jnp.dot(table[pl.ds(0, ROWS), :], wself[...], preferred_element_type=F32)
    pre = pre + jnp.dot(pair[1], wneigh[...], preferred_element_type=F32)
    sig = jax.nn.sigmoid(pre)
    layer[...] = (pre * sig).astype(BF16)
    act[...] = (ograd[...].astype(F32) * sig * (1.0 + pre * (1.0 - sig))).astype(BF16)

    mine = core * ROWS
    other = ROWS - mine

    def cols(c):
        return pl.ds(sum(WIDTHS[:c]), WIDTHS[c])

    def remote(src, dst, send_sem, recv_sem, device):
        copy = pltpu.make_async_remote_copy(
            src_ref=src, dst_ref=dst, send_sem=send_sem, recv_sem=recv_sem,
            device_id=device, device_id_type=MESH,
        )
        copy.start()

    def wait_for(ref, sem):
        pltpu.make_async_copy(ref, ref, sem).wait()

    pl.semaphore_wait(barrier, len(peers))
    for c in range(CH):
        wpart[1, :, cols(c)] = lax.dot_general(
            pair[1 - core], act[:, cols(c)], DIM0, preferred_element_type=F32
        )
        remote(wpart.at[1, :, cols(c)], crecv.at[:, cols(c)], cs.at[c], cr.at[c], at_core())
    wpart[0] = lax.dot_general(pair[core], act[...], DIM0, preferred_element_type=F32)

    for c in range(CH):
        wait_for(crecv.at[:, cols(c)], cr.at[c])
        total = wpart[0, :, cols(c)] + crecv[:, cols(c)]
        s1[:, cols(c)] = total
        xsend[:, cols(c)] = total.astype(BF16)
        for k in FAR_X:
            to = lax.rem(g + k, NX)
            rows = pl.ds(pl.multiple_of(to * XB, XB), XB)
            remote(xsend.at[rows, cols(c)], xrecv.at[k - 1, :, cols(c)], xs.at[c], xr.at[c], at_x(k))

    copies[7].wait()
    copies[8].wait()
    own_ids = lax.broadcasted_iota(jnp.int32, (ROWS, ROWS), 0)
    select[...] = jnp.where(own_ids == send[...], 1.0, 0.0).astype(BF16)
    sent[...] = lax.dot_general(
        select[...], table[pl.ds(0, ROWS), :], DIM0, preferred_element_type=F32
    ).astype(BF16)
    here = pl.ds(pl.multiple_of(g * XB, XB), XB)
    for k in range(1, NX):
        to = lax.rem(g + k, NX)
        rows = pl.ds(pl.multiple_of(to * XB, XB), XB)
        remote(sent.at[rows], nhalo.at[here], hs, hr, at_x(k))
    own_sent = pltpu.make_async_copy(sent.at[here], nhalo.at[here], osem.at[0])
    own_sent.start()

    grad = lax.dot_general(act[...], wneigh[...], DIM1, preferred_element_type=F32)
    grad = grad * (1.0 / FAN)
    high = grad.astype(BF16)
    low = (grad - high.astype(F32)).astype(BF16)
    halo_counts = counts[pl.ds(ROWS, ROWS), :]
    back = jnp.dot(halo_counts, high, preferred_element_type=F32)
    back = back + jnp.dot(halo_counts, low, preferred_element_type=F32)
    hgrad[...] = back.astype(BF16)
    for k in range(1, NX):
        to = lax.rem(g + k, NX)
        rows = pl.ds(pl.multiple_of(to * XB, XB), XB)
        remote(hgrad.at[rows], nghalo.at[here], gs, gr, at_x(k))
    own_grad = pltpu.make_async_copy(hgrad.at[here], nghalo.at[here], osem.at[1])
    own_grad.start()

    for c in range(CH):
        wait_for(xrecv.at[:, :, cols(c)], xr.at[c])
        total = s1[here, cols(c)]
        for k in range(NX - 1):
            total = total + xrecv[k, :, cols(c)].astype(F32)
        s2[:, cols(c)] = total
        ysend[:, cols(c)] = total.astype(BF16)
        for k in FAR_Y:
            to = lax.rem(y + k, NY)
            rows = pl.ds(pl.multiple_of(to * YB, YB), YB)
            remote(
                ysend.at[rows, cols(c)], yrecv.at[pl.ds((k - 1) * YB, YB), cols(c)],
                ys.at[c], yr.at[c], at_y(k),
            )

    own_y = pl.ds(pl.multiple_of(y * YB, YB), YB)
    own_z = pl.ds(pl.multiple_of(z * YB, YB), YB)
    for c in range(CH):
        wait_for(yrecv.at[:, cols(c)], yr.at[c])
        total = s2[own_y, cols(c)]
        for k in range(NY - 1):
            total = total + yrecv[pl.ds(k * YB, YB), cols(c)].astype(F32)
        zbuf[own_z, cols(c)] = total.astype(BF16)
        for k in range(1, FIRST + 1):
            remote(zbuf.at[own_z, cols(c)], zbuf.at[own_z, cols(c)], zs.at[c], zr.at[c], at_z(k))
    for c in range(CH):
        for k in range(FIRST + 1, NZ):
            remote(zbuf.at[own_z, cols(c)], zbuf.at[own_z, cols(c)], zs.at[c], zr.at[c], at_z(k))

    own = lax.dot_general(act[...], wself[...], DIM1, preferred_element_type=F32)
    own_counts = counts[pl.ds(0, ROWS), :]
    own = own + jnp.dot(own_counts, high, preferred_element_type=F32)
    own = own + jnp.dot(own_counts, low, preferred_element_type=F32)
    own = own + jnp.dot(select[...], gin[...], preferred_element_type=F32)
    fgrad[...] = own.astype(BF16)

    row_y = pl.ds(pl.multiple_of(mine + g * XB + y * YB, YB), YB)
    row_x = pl.ds(pl.multiple_of(mine + g * XB, XB), XB)
    row_c = pl.ds(pl.multiple_of(mine, ROWS), ROWS)
    row_o = pl.ds(pl.multiple_of(other, ROWS), ROWS)
    for c in range(CH):
        wait_for(zbuf.at[pl.ds(0, (NZ - 1) * YB), cols(c)], zr.at[c])
        total = zbuf[pl.ds(0, YB), cols(c)].astype(F32)
        for k in range(1, NZ):
            total = total + zbuf[pl.ds(k * YB, YB), cols(c)].astype(F32)
        ag[row_y, cols(c)] = (total * scale).astype(BF16)
        for k in FAR_Y:
            remote(
                ag.at[row_y, cols(c)], ag.at[row_y, cols(c)], ays.at[c], ayr.at[c], at_y(k)
            )
    for c in range(CH):
        wait_for(ag.at[pl.ds(0, (NY - 1) * YB), cols(c)], ayr.at[c])
        for k in FAR_X:
            remote(
                ag.at[row_x, cols(c)], ag.at[row_x, cols(c)], axs.at[c], axr.at[c], at_x(k)
            )
    for c in range(CH):
        wait_for(ag.at[pl.ds(0, (NX - 1) * XB), cols(c)], axr.at[c])
        remote(ag.at[row_c, cols(c)], ag.at[row_c, cols(c)], acs.at[c], acr.at[c], at_core())
    for c in range(CH):
        wait_for(ag.at[row_o, cols(c)], acr.at[c])

    wait_for(nhalo.at[pl.ds(0, ROWS - XB)], hr)
    wait_for(nghalo.at[pl.ds(0, ROWS - XB)], gr)
    wait_for(sent.at[pl.ds(0, ROWS - XB)], hs)
    wait_for(hgrad.at[pl.ds(0, ROWS - XB)], gs)
    for c in range(CH):
        wait_for(crecv.at[:, cols(c)], cs.at[c])
        wait_for(xrecv.at[:, :, cols(c)], xs.at[c])
        wait_for(yrecv.at[:, cols(c)], ys.at[c])
        wait_for(zbuf.at[pl.ds(0, (NZ - 1) * YB), cols(c)], zs.at[c])
        wait_for(ag.at[pl.ds(0, (NY - 1) * YB), cols(c)], ays.at[c])
        wait_for(ag.at[pl.ds(0, (NX - 1) * XB), cols(c)], axs.at[c])
        wait_for(ag.at[row_c, cols(c)], acs.at[c])
    for copy in (own_sent, own_grad):
        copy.wait()


def deliver(layer, fgrad, nhalo, nghalo, ag, o_layer, o_fgrad, o_nhalo, o_nghalo, o_w, wide, sems, wsems):
    pairs = ((layer, o_layer), (fgrad, o_fgrad), (nhalo, o_nhalo), (nghalo, o_nghalo))
    copies = [pltpu.make_async_copy(s, d, sems.at[i]) for i, (s, d) in enumerate(pairs)]
    for copy in copies:
        copy.start()
    pieces = wsems.shape[1]
    size = ROWS // pieces
    for m in range(2):
        for q in range(pieces):
            rows = pl.ds(q * size, size)
            wide[m, rows, :] = ag[pl.ds(m * ROWS + q * size, size), :].astype(F32)
            copies.append(
                pltpu.make_async_copy(wide.at[m, rows], o_w.at[m, rows], wsems.at[m, q])
            )
            copies[-1].start()
    for copy in copies:
        copy.wait()


def body(features, halo_in, neighbors, send_rows, grad_halo_in, out_grad, w_self, w_neigh):
    total_nodes = ROWS * lax.axis_size("dom") * lax.axis_size("grp")
    scale = 1.0 / math.sqrt(total_nodes)
    inside = pl.BlockSpec(memory_space=pltpu.VMEM)
    outside = pl.BlockSpec(memory_space=pltpu.HBM)
    half = pltpu.VMEM((ROWS, H), BF16)
    dma = pltpu.SemaphoreType.DMA
    args = [
        features, halo_in, neighbors.T, send_rows.reshape(1, ROWS), grad_halo_in, out_grad,
        w_self, w_neigh,
    ]
    results = pl.pallas_call(
        functools.partial(kernel, scale),
        out_shape=(half, half, half, half, pltpu.VMEM((2 * ROWS, H), BF16)),
        in_specs=[outside] * 8,
        out_specs=(inside,) * 5,
        scratch_shapes=[
            pltpu.VMEM((2 * ROWS, H), BF16),
            pltpu.VMEM((2, ROWS, H), BF16),
            pltpu.VMEM((FAN, ROWS), jnp.int32),
            pltpu.VMEM((1, ROWS), jnp.int32),
            half, half, half, half,
            pltpu.VMEM((2 * ROWS, ROWS), BF16),
            half, half, half, half,
            pltpu.VMEM((2, ROWS, H), F32),
            pltpu.VMEM((ROWS, H), F32),
            pltpu.VMEM((ROWS, H), F32),
            half,
            pltpu.VMEM((NX - 1, XB, H), BF16),
            pltpu.VMEM((XB, H), F32),
            pltpu.VMEM((XB, H), BF16),
            pltpu.VMEM(((NY - 1) * YB, H), BF16),
            pltpu.VMEM((NZ * YB, H), BF16),
            dma((9,)), dma((2,)),
        ] + [dma((CH,))] * 14 + [dma] * 4,
        compiler_params=pltpu.CompilerParams(
            collective_id=0, has_side_effects=True, vmem_limit_bytes=48 << 20
        ),
    )(*[pltpu.with_memory_space_constraint(a, pltpu.HBM) for a in args])
    rows = jax.ShapeDtypeStruct((ROWS, H), BF16)
    pieces = 4
    return pl.pallas_call(
        deliver,
        out_shape=(rows, rows, rows, rows, jax.ShapeDtypeStruct((2, ROWS, H), F32)),
        in_specs=[inside] * 5,
        out_specs=(outside,) * 5,
        scratch_shapes=[pltpu.VMEM((2, ROWS, H), F32), dma((4,)), dma((2, pieces))],
        compiler_params=pltpu.CompilerParams(vmem_limit_bytes=16 << 20),
    )(*[pltpu.with_memory_space_constraint(a, pltpu.VMEM) for a in results])


def solution(mesh):
    rows = P(("dom", "grp"), None)
    return jax.shard_map(
        body,
        mesh=mesh,
        in_specs=(rows, rows, rows, P(("dom", "grp")), rows, rows, P(), P()),
        out_specs=(rows, rows, rows, rows, P()),
        check_vma=False,
    )
```

```python
import functools
import math

import jax
import jax.numpy as jnp
from jax import lax
from jax.experimental import pallas as pl
from jax.experimental.pallas import tpu as pltpu
from jax.sharding import PartitionSpec as P

MESH = pl.DeviceIdType.MESH
NX, NY, NZ = 4, 8, 12
ROWS = 512
H = 512
FAN = 10
XB = ROWS // NX
YB = XB // NY
WIDTHS = (128, 256, 128)
CH = len(WIDTHS)
FIRST = 2
FAR_X = (2, 1, 3)
FAR_Y = (4, 3, 5, 2, 6, 1, 7)
DIM0 = (((0,), (0,)), ((), ()))
DIM1 = (((1,), (1,)), ((), ()))
F32 = jnp.float32
BF16 = jnp.bfloat16


def kernel(
    scale,
    feat_hbm, halo_hbm, nbr_hbm, send_hbm, gin_hbm, ograd_hbm, ws_hbm, wn_hbm,
    layer, fgrad, nhalo, nghalo, ag,
    table, pair, nbr, send, gin, ograd, wself, wneigh,
    counts, select, act, hgrad, sent,
    wpart, crecv, s1, xsend, xrecv, s2, ysend, yrecv, zbuf,
    lsem, osem, cs, cr, xs, xr, ys, yr, zs, zr, ays, ayr, axs, axr, acs, acr, hs, hr, gs, gr,
):
    dom = lax.axis_index("dom")
    g = lax.axis_index("grp")
    core = lax.rem(dom, 2)
    y = lax.rem(dom // 2, NY)
    z = dom // (2 * NY)

    def at_core():
        return (dom + 1 - 2 * core, g)

    def at_x(k):
        return (dom, lax.rem(g + k, NX))

    def at_y(k):
        return ((z * NY + lax.rem(y + k, NY)) * 2 + core, g)

    def at_z(k):
        to = jnp.where(z >= k, k - 1, k)
        return ((to * NY + y) * 2 + core, g)

    barrier = pltpu.get_barrier_semaphore()
    peers = [at_core()] + [at_x(k) for k in range(1, NX)]
    peers += [at_y(k) for k in range(1, NY)] + [at_z(k) for k in range(1, NZ)]
    loads = [
        (nbr_hbm, nbr),
        (feat_hbm, table.at[pl.ds(0, ROWS)]),
        (halo_hbm, table.at[pl.ds(ROWS, ROWS)]),
        (ws_hbm, wself),
        (wn_hbm, wneigh),
        (ograd_hbm, ograd),
        (feat_hbm, pair.at[0]),
        (send_hbm, send),
        (gin_hbm, gin),
    ]
    copies = [pltpu.make_async_copy(s, d, lsem.at[i]) for i, (s, d) in enumerate(loads)]
    for copy in copies:
        copy.start()
    for peer in peers:
        pl.semaphore_signal(barrier, inc=1, device_id=peer, device_id_type=MESH)

    copies[0].wait()
    one = jnp.full((16, ROWS), 1, jnp.int16)
    none = jnp.zeros((16, ROWS), jnp.int16)
    slots = [
        jnp.broadcast_to(nbr[pl.ds(k, 1), :], (16, ROWS)).astype(jnp.int16) for k in range(FAN)
    ]
    ids = lax.broadcasted_iota(jnp.int32, (16, 128), 0)
    GROUP = 128

    @pl.loop(0, 2 * ROWS // GROUP)
    def _(b):
        for part in range(GROUP // 16):
            first = pl.multiple_of(b * GROUP + part * 16, 16)
            row_ids = jnp.tile((ids + first).astype(jnp.int16), (1, ROWS // 128))
            total = none
            for slot in slots:
                total = total + jnp.where(slot == row_ids, one, none)
            counts[pl.ds(first, 16), :] = total.astype(BF16)

    for i in (1, 2, 3, 4, 5, 6):
        copies[i].wait()
    agg = lax.dot_general(counts[...], table[...], DIM0, preferred_element_type=F32) * (1.0 / FAN)
    pair[1] = agg.astype(BF16)
    pre = jnp.dot(table[pl.ds(0, ROWS), :], wself[...], preferred_element_type=F32)
    pre = pre + jnp.dot(pair[1], wneigh[...], preferred_element_type=F32)
    sig = jax.nn.sigmoid(pre)
    layer[...] = (pre * sig).astype(BF16)
    act[...] = (ograd[...].astype(F32) * sig * (1.0 + pre * (1.0 - sig))).astype(BF16)

    mine = core * ROWS
    other = ROWS - mine

    def cols(c):
        return pl.ds(sum(WIDTHS[:c]), WIDTHS[c])

    def remote(src, dst, send_sem, recv_sem, device):
        copy = pltpu.make_async_remote_copy(
            src_ref=src, dst_ref=dst, send_sem=send_sem, recv_sem=recv_sem,
            device_id=device, device_id_type=MESH,
        )
        copy.start()

    def wait_for(ref, sem):
        pltpu.make_async_copy(ref, ref, sem).wait()

    pl.semaphore_wait(barrier, len(peers))
    for c in range(CH):
        wpart[1, :, cols(c)] = lax.dot_general(
            pair[1 - core], act[:, cols(c)], DIM0, preferred_element_type=F32
        )
        remote(wpart.at[1, :, cols(c)], crecv.at[:, cols(c)], cs.at[c], cr.at[c], at_core())
    wpart[0] = lax.dot_general(pair[core], act[...], DIM0, preferred_element_type=F32)

    for c in range(CH):
        wait_for(crecv.at[:, cols(c)], cr.at[c])
        total = wpart[0, :, cols(c)] + crecv[:, cols(c)]
        s1[:, cols(c)] = total
        xsend[:, cols(c)] = total.astype(BF16)
        for k in FAR_X:
            to = lax.rem(g + k, NX)
            rows = pl.ds(pl.multiple_of(to * XB, XB), XB)
            remote(xsend.at[rows, cols(c)], xrecv.at[k - 1, :, cols(c)], xs.at[c], xr.at[c], at_x(k))

    copies[7].wait()
    copies[8].wait()
    own_ids = lax.broadcasted_iota(jnp.int32, (ROWS, ROWS), 0)
    select[...] = jnp.where(own_ids == send[...], 1.0, 0.0).astype(BF16)
    sent[...] = lax.dot_general(
        select[...], table[pl.ds(0, ROWS), :], DIM0, preferred_element_type=F32
    ).astype(BF16)
    here = pl.ds(pl.multiple_of(g * XB, XB), XB)
    for k in range(1, NX):
        to = lax.rem(g + k, NX)
        rows = pl.ds(pl.multiple_of(to * XB, XB), XB)
        remote(sent.at[rows], nhalo.at[here], hs, hr, at_x(k))
    own_sent = pltpu.make_async_copy(sent.at[here], nhalo.at[here], osem.at[0])
    own_sent.start()

    grad = lax.dot_general(act[...], wneigh[...], DIM1, preferred_element_type=F32)
    grad = grad * (1.0 / FAN)
    high = grad.astype(BF16)
    low = (grad - high.astype(F32)).astype(BF16)
    halo_counts = counts[pl.ds(ROWS, ROWS), :]
    back = jnp.dot(halo_counts, high, preferred_element_type=F32)
    back = back + jnp.dot(halo_counts, low, preferred_element_type=F32)
    hgrad[...] = back.astype(BF16)
    for k in range(1, NX):
        to = lax.rem(g + k, NX)
        rows = pl.ds(pl.multiple_of(to * XB, XB), XB)
        remote(hgrad.at[rows], nghalo.at[here], gs, gr, at_x(k))
    own_grad = pltpu.make_async_copy(hgrad.at[here], nghalo.at[here], osem.at[1])
    own_grad.start()

    for c in range(CH):
        wait_for(xrecv.at[:, :, cols(c)], xr.at[c])
        total = s1[here, cols(c)]
        for k in range(NX - 1):
            total = total + xrecv[k, :, cols(c)].astype(F32)
        s2[:, cols(c)] = total
        ysend[:, cols(c)] = total.astype(BF16)
        for k in FAR_Y:
            to = lax.rem(y + k, NY)
            rows = pl.ds(pl.multiple_of(to * YB, YB), YB)
            remote(
                ysend.at[rows, cols(c)], yrecv.at[pl.ds((k - 1) * YB, YB), cols(c)],
                ys.at[c], yr.at[c], at_y(k),
            )

    own_y = pl.ds(pl.multiple_of(y * YB, YB), YB)
    own_z = pl.ds(pl.multiple_of(z * YB, YB), YB)
    for c in range(CH):
        wait_for(yrecv.at[:, cols(c)], yr.at[c])
        total = s2[own_y, cols(c)]
        for k in range(NY - 1):
            total = total + yrecv[pl.ds(k * YB, YB), cols(c)].astype(F32)
        zbuf[own_z, cols(c)] = total.astype(BF16)
        for k in range(1, FIRST + 1):
            remote(zbuf.at[own_z, cols(c)], zbuf.at[own_z, cols(c)], zs.at[c], zr.at[c], at_z(k))
    for c in range(CH):
        for k in range(FIRST + 1, NZ):
            remote(zbuf.at[own_z, cols(c)], zbuf.at[own_z, cols(c)], zs.at[c], zr.at[c], at_z(k))

    own = lax.dot_general(act[...], wself[...], DIM1, preferred_element_type=F32)
    own_counts = counts[pl.ds(0, ROWS), :]
    own = own + jnp.dot(own_counts, high, preferred_element_type=F32)
    own = own + jnp.dot(own_counts, low, preferred_element_type=F32)
    own = own + jnp.dot(select[...], gin[...], preferred_element_type=F32)
    fgrad[...] = own.astype(BF16)

    row_y = pl.ds(pl.multiple_of(mine + g * XB + y * YB, YB), YB)
    row_x = pl.ds(pl.multiple_of(mine + g * XB, XB), XB)
    row_c = pl.ds(pl.multiple_of(mine, ROWS), ROWS)
    row_o = pl.ds(pl.multiple_of(other, ROWS), ROWS)
    for c in range(CH):
        wait_for(zbuf.at[pl.ds(0, (NZ - 1) * YB), cols(c)], zr.at[c])
        total = zbuf[pl.ds(0, YB), cols(c)].astype(F32)
        for k in range(1, NZ):
            total = total + zbuf[pl.ds(k * YB, YB), cols(c)].astype(F32)
        ag[row_y, cols(c)] = (total * scale).astype(BF16)
        for k in FAR_Y:
            remote(
                ag.at[row_y, cols(c)], ag.at[row_y, cols(c)], ays.at[c], ayr.at[c], at_y(k)
            )
    for c in range(CH):
        wait_for(ag.at[pl.ds(0, (NY - 1) * YB), cols(c)], ayr.at[c])
        for k in FAR_X:
            remote(
                ag.at[row_x, cols(c)], ag.at[row_x, cols(c)], axs.at[c], axr.at[c], at_x(k)
            )
    for c in range(CH):
        wait_for(ag.at[pl.ds(0, (NX - 1) * XB), cols(c)], axr.at[c])
        remote(ag.at[row_c, cols(c)], ag.at[row_c, cols(c)], acs.at[c], acr.at[c], at_core())
    for c in range(CH):
        wait_for(ag.at[row_o, cols(c)], acr.at[c])

    wait_for(nhalo.at[pl.ds(0, ROWS - XB)], hr)
    wait_for(nghalo.at[pl.ds(0, ROWS - XB)], gr)
    wait_for(sent.at[pl.ds(0, ROWS - XB)], hs)
    wait_for(hgrad.at[pl.ds(0, ROWS - XB)], gs)
    for c in range(CH):
        wait_for(crecv.at[:, cols(c)], cs.at[c])
        wait_for(xrecv.at[:, :, cols(c)], xs.at[c])
        wait_for(yrecv.at[:, cols(c)], ys.at[c])
        wait_for(zbuf.at[pl.ds(0, (NZ - 1) * YB), cols(c)], zs.at[c])
        wait_for(ag.at[pl.ds(0, (NY - 1) * YB), cols(c)], ays.at[c])
        wait_for(ag.at[pl.ds(0, (NX - 1) * XB), cols(c)], axs.at[c])
        wait_for(ag.at[row_c, cols(c)], acs.at[c])
    for copy in (own_sent, own_grad):
        copy.wait()


def deliver(layer, fgrad, nhalo, nghalo, ag, o_layer, o_fgrad, o_nhalo, o_nghalo, o_w, wide, sems, wsems):
    pairs = ((layer, o_layer), (fgrad, o_fgrad), (nhalo, o_nhalo), (nghalo, o_nghalo))
    copies = [pltpu.make_async_copy(s, d, sems.at[i]) for i, (s, d) in enumerate(pairs)]
    for copy in copies:
        copy.start()
    pieces = wsems.shape[1]
    size = ROWS // pieces
    for m in range(2):
        for q in range(pieces):
            rows = pl.ds(q * size, size)
            wide[m, rows, :] = ag[pl.ds(m * ROWS + q * size, size), :].astype(F32)
            copies.append(
                pltpu.make_async_copy(wide.at[m, rows], o_w.at[m, rows], wsems.at[m, q])
            )
            copies[-1].start()
    for copy in copies:
        copy.wait()


def body(features, halo_in, neighbors, send_rows, grad_halo_in, out_grad, w_self, w_neigh):
    total_nodes = ROWS * lax.axis_size("dom") * lax.axis_size("grp")
    scale = 1.0 / math.sqrt(total_nodes)
    inside = pl.BlockSpec(memory_space=pltpu.VMEM)
    outside = pl.BlockSpec(memory_space=pltpu.HBM)
    half = pltpu.VMEM((ROWS, H), BF16)
    dma = pltpu.SemaphoreType.DMA
    args = [
        features, halo_in, neighbors.T, send_rows.reshape(1, ROWS), grad_halo_in, out_grad,
        w_self, w_neigh,
    ]
    results = pl.pallas_call(
        functools.partial(kernel, scale),
        out_shape=(half, half, half, half, pltpu.VMEM((2 * ROWS, H), BF16)),
        in_specs=[outside] * 8,
        out_specs=(inside,) * 5,
        scratch_shapes=[
            pltpu.VMEM((2 * ROWS, H), BF16),
            pltpu.VMEM((2, ROWS, H), BF16),
            pltpu.VMEM((FAN, ROWS), jnp.int32),
            pltpu.VMEM((1, ROWS), jnp.int32),
            half, half, half, half,
            pltpu.VMEM((2 * ROWS, ROWS), BF16),
            half, half, half, half,
            pltpu.VMEM((2, ROWS, H), F32),
            pltpu.VMEM((ROWS, H), F32),
            pltpu.VMEM((ROWS, H), F32),
            half,
            pltpu.VMEM((NX - 1, XB, H), BF16),
            pltpu.VMEM((XB, H), F32),
            pltpu.VMEM((XB, H), BF16),
            pltpu.VMEM(((NY - 1) * YB, H), BF16),
            pltpu.VMEM((NZ * YB, H), BF16),
            dma((9,)), dma((2,)),
        ] + [dma((CH,))] * 14 + [dma] * 4,
        compiler_params=pltpu.CompilerParams(
            collective_id=0, has_side_effects=True, vmem_limit_bytes=48 << 20
        ),
    )(*[pltpu.with_memory_space_constraint(a, pltpu.HBM) for a in args])
    rows = jax.ShapeDtypeStruct((ROWS, H), BF16)
    pieces = 4
    return pl.pallas_call(
        deliver,
        out_shape=(rows, rows, rows, rows, jax.ShapeDtypeStruct((2, ROWS, H), F32)),
        in_specs=[inside] * 5,
        out_specs=(outside,) * 5,
        scratch_shapes=[pltpu.VMEM((2, ROWS, H), F32), dma((4,)), dma((2, pieces))],
        compiler_params=pltpu.CompilerParams(vmem_limit_bytes=16 << 20),
    )(*[pltpu.with_memory_space_constraint(a, pltpu.VMEM) for a in results])


def solution(mesh):
    rows = P(("dom", "grp"), None)
    return jax.shard_map(
        body,
        mesh=mesh,
        in_specs=(rows, rows, rows, P(("dom", "grp")), rows, rows, P(), P()),
        out_specs=(rows, rows, rows, rows, P()),
        check_vma=False,
    )
```
